32 devices in a mesh: dom: 8 (over z, y), sub: 4 (over x, core).
Axes of the slice: x: 2, y: 2, z: 4, core: 2. Of those that a mesh axis runs over, the one named last changes fastest.
Arguments:
- rhs: float32 [5, 64, 4096], P(None, 'sub', 'dom'), may hold values from -0.4 to 0.4
- lateral: float32 [5, 64, 4096], P(None, 'sub', 'dom'), may hold values from 0.05 to 0.5
- piece_line: int32 [4, 4096], P('sub', 'dom'), may hold values from 0 to 4095, as said below
- lower: float32 [5, 5, 64, 4096], P(None, None, None, ('dom', 'sub'))
- diag_blocks: float32 [5, 5, 64, 4096], P(None, None, None, ('dom', 'sub')), as said below
- upper: float32 [5, 5, 64, 4096], P(None, None, None, ('dom', 'sub'))
Outputs:
- correction: float32 [5, 64, 4096], P(None, 'sub', 'dom')
The draws below stay inside these ranges and needn't reach their ends.
Inputs may be any that keep to these rules, and one draw needn't show every extreme that they name: For each s, piece_line[s] holds every line id once. The owner of a line is line // 512; the 512 slots of one index of dom hold at most 96 pieces of one owner's lines, and some hold exactly 96. Every block row of the three arrays is diagonally dominant: the diagonal entry of diag_blocks exceeds the sum of magnitudes of the other entries of its row in all three.
All inputs are finite; a program needn't handle non-finite values.
Results may differ from the reference program's by a relative error of at most 0.00002.
Values sent between devices are 32-bit elements; how exact they have to be, the bound alone decides.
A program may use at most 64 MiB of HBM per device.

```python
import math
import jax
import jax.numpy as jnp
from jax import lax

FIELDS = 5
LINE_LEN = 64
LINE_DEV = 512
SUBPARTS = 4
PIECE = 16
LINES = 4096
CAP = 96


def line_blocks(key):
    shape = (FIELDS, FIELDS, LINE_LEN, LINES)
    keys = [jax.random.fold_in(key, 11 + k) for k in range(6)]
    spread = 0.1
    dia_lo = -1.2
    dia_hi = -0.6
    eye = jnp.eye(FIELDS, dtype=jnp.float32)[:, :, None, None]

    def side(first_key, second_key):
        offdiag = jax.random.uniform(first_key, shape, jnp.float32, -spread, spread)
        ondiag = jax.random.uniform(second_key, shape, jnp.float32, dia_lo, dia_hi)
        return offdiag * (1.0 - eye) + ondiag * eye
    low = side(keys[0], keys[1])
    high = side(keys[2], keys[3])
    own_off = jax.random.uniform(keys[4], shape, jnp.float32, -0.15, 0.15) * (1.0 - eye)
    margin = jnp.exp(jax.random.uniform(keys[5], (FIELDS, LINE_LEN, LINES), jnp.float32, math.log(0.0005), math.log(0.004)))
    dominant = jnp.sum(jnp.abs(low), axis=1) + jnp.sum(jnp.abs(high), axis=1) + jnp.sum(jnp.abs(own_off), axis=1) + margin
    middle = own_off + eye * dominant[:, None]
    return (low, middle, high)


def draw_lower(key, part):
    return line_blocks(key)[0]


def draw_diag_blocks(key, part):
    return line_blocks(key)[1]


def draw_upper(key, part):
    return line_blocks(key)[2]


def draw_piece_line(key, part):
    number = LINES // LINE_DEV
    mean_load = LINE_DEV // number
    least = 2 * mean_load - CAP
    slots = jnp.arange(LINE_DEV, dtype=jnp.int32)
    sources = jnp.arange(number, dtype=jnp.int32)
    layers = []
    for s in range(SUBPARTS):
        base = jax.random.fold_in(key, 100 + s)
        order = jax.random.permutation(jax.random.fold_in(base, 1), number)
        extra = jax.random.randint(jax.random.fold_in(base, 2), (number // 2,), least, CAP + 1).at[0].set(least)
        weights = jnp.zeros((number,), jnp.int32).at[order[0::2]].set(2 * mean_load - extra).at[order[1::2]].set(extra)
        ends = jnp.cumsum(weights)
        offset = jnp.sum((slots[:, None] >= ends[None, :]).astype(jnp.int32), axis=1)
        ranking = jax.random.permutation(jax.random.fold_in(base, 3), number)
        owner = ranking[(sources[:, None] + offset[None, :]) % number]
        line = owner * LINE_DEV + slots[None, :]
        scores = jax.random.randint(jax.random.fold_in(base, 4), (number, LINE_DEV), 0, 1 << 20) * LINE_DEV + slots[None, :]
        shuffle = jnp.argsort(scores, axis=1)
        layers.append(jnp.take_along_axis(line, shuffle, axis=1).reshape(LINES))
    return jnp.stack(layers).astype(jnp.int32)


def shard_levels(rng, extent, cuts, low, largest):
    gain = 1.0
    for dim, blocks in cuts:
        heights = jax.random.uniform(jax.random.fold_in(jax.random.fold_in(rng, 6), dim), (blocks,), jnp.float32, low / len(cuts), largest / len(cuts))
        gain = gain * jnp.repeat(jnp.exp(heights), extent[dim] // blocks).reshape((-1,) + (1,) * (len(extent) - 1 - dim))
    return gain


def noise(key, extent, scale, reach, split=(), kind=jnp.bfloat16):
    entries = scale * jax.random.normal(key, extent, jnp.float32)
    if split:
        entries = entries * shard_levels(key, extent, split, -0.22, 0.18)
    return jnp.clip(entries, -reach, reach).astype(kind)


def setup_inputs(seed: int = 0) -> dict:
    key_of = jax.random.split(jax.random.key(seed), 7)
    return {
        "rhs": noise(key_of[0], (FIELDS, LINE_LEN, LINES), 0.05, 0.4, ((1, 4), (2, 8)), jnp.float32),
        "lateral": jnp.clip(jnp.exp(math.log(0.5) - 2.3025851 * jax.random.uniform(key_of[1], (FIELDS, LINE_LEN, LINES), jnp.float32) ** shard_levels(key_of[1], (FIELDS, LINE_LEN, LINES), ((1, 4), (2, 8)), -0.2, 0.2)), 0.05, 0.5),
        "piece_line": draw_piece_line(jax.random.fold_in(key_of[6], 71), 0),
        "lower": draw_lower(jax.random.fold_in(key_of[6], 71), 0),
        "diag_blocks": draw_diag_blocks(jax.random.fold_in(key_of[6], 71), 0),
        "upper": draw_upper(jax.random.fold_in(key_of[6], 71), 0),
    }


def matmul_five(left, right):
    return jnp.sum(left[:, :, None] * right[None, :, :], axis=1)


def matvec_five(left, vector):
    return jnp.sum(left * vector[None], axis=1)


def invert_five(matrix):
    work = matrix
    eye_shape = (5, 5) + (1,) * (matrix.ndim - 2)
    inverse = jnp.broadcast_to(jnp.eye(5, dtype=matrix.dtype).reshape(eye_shape), matrix.shape)
    for k in range(5):
        pivot = 1.0 / work[k, k]
        row_work = work[k] * pivot
        row_inv = inverse[k] * pivot
        factor = work[:, k]
        work = work - factor[:, None] * row_work[None]
        inverse = inverse - factor[:, None] * row_inv[None]
        work = work.at[k].set(row_work)
        inverse = inverse.at[k].set(row_inv)
    return inverse


def shift_down(array, axis):
    first = lax.slice_in_dim(array, 1, array.shape[axis], axis=axis)
    zeros = jnp.zeros_like(lax.slice_in_dim(array, 0, 1, axis=axis))
    return jnp.concatenate([first, zeros], axis=axis)


def shift_up(array, axis):
    last = lax.slice_in_dim(array, 0, array.shape[axis] - 1, axis=axis)
    zeros = jnp.zeros_like(lax.slice_in_dim(array, 0, 1, axis=axis))
    return jnp.concatenate([zeros, last], axis=axis)


def reduce_solve(low, mid, high, values):
    count = mid.shape[2]
    if count == 1:
        return matvec_five(invert_five(mid), values)
    low_even, low_odd = low[:, :, 0::2], low[:, :, 1::2]
    mid_even, mid_odd = mid[:, :, 0::2], mid[:, :, 1::2]
    high_even, high_odd = high[:, :, 0::2], high[:, :, 1::2]
    val_even, val_odd = values[:, 0::2], values[:, 1::2]
    inv_even = invert_five(mid_even)
    inv_next = shift_down(inv_even, 2)
    low_next = shift_down(low_even, 2)
    high_next = shift_down(high_even, 2)
    val_next = shift_down(val_even, 1)
    alpha = -matmul_five(low_odd, inv_even)
    gamma = -matmul_five(high_odd, inv_next)
    mid_new = mid_odd + matmul_five(alpha, high_even) + matmul_five(gamma, low_next)
    low_new = matmul_five(alpha, low_even)
    high_new = matmul_five(gamma, high_next)
    val_new = val_odd + matvec_five(alpha, val_even) + matvec_five(gamma, val_next)
    x_odd = reduce_solve(low_new, mid_new, high_new, val_new)
    x_prev = shift_up(x_odd, 1)
    x_even = matvec_five(inv_even, val_even - matvec_five(low_even, x_prev) - matvec_five(high_even, x_odd))
    both = jnp.stack([x_even, x_odd], axis=2)
    return both.reshape(values.shape)


def reference(rhs, lateral, piece_line, lower, diag_blocks, upper):
    def to_lines(field):
        result = jnp.zeros_like(field)
        for s in range(SUBPARTS):
            result = result.at[:, s * PIECE:(s + 1) * PIECE, piece_line[s]].set(field[:, s * PIECE:(s + 1) * PIECE, :])
        return result

    def to_pieces(lines):
        pieces = [lines[:, s * PIECE:(s + 1) * PIECE][:, :, piece_line[s]] for s in range(SUBPARTS)]
        return jnp.concatenate(pieces, axis=1)

    def solve_all(values):
        number = LINES // LINE_DEV

        def one_block(index):
            start = index * LINE_DEV

            def take(array):
                return lax.dynamic_slice_in_dim(array, start, LINE_DEV, array.ndim - 1)

            return reduce_solve(take(lower), take(diag_blocks), take(upper), take(values))

        blocks = lax.map(one_block, jnp.arange(number, dtype=jnp.int32))
        return jnp.transpose(blocks, (1, 2, 0, 3)).reshape(FIELDS, LINE_LEN, LINES)

    first = to_pieces(solve_all(to_lines(rhs)))
    padded = jnp.pad(first, ((0, 0), (0, 0), (1, 1)))
    residual = rhs + lateral * (padded[:, :, :-2] + padded[:, :, 2:])
    return to_pieces(solve_all(to_lines(residual)))
```

```python
import functools

import jax
import jax.numpy as jnp
from jax import lax
from jax.experimental import pallas as pl
from jax.experimental.pallas import tpu as pltpu
from jax.sharding import PartitionSpec as P

F = 5
VMEM = pl.BlockSpec(memory_space=pltpu.VMEM)
PARAMS = pltpu.CompilerParams(vmem_limit_bytes=40 * 1024 * 1024)
NT = (((1,), (1,)), ((), ()))
NN = (((1,), (0,)), ((), ()))


def dot(left, right, dims):
    return lax.dot_general(
        left, right, dims, precision=lax.Precision.HIGHEST, preferred_element_type=jnp.float32
    )


def call(kernel, outs, *args, scratch=()):
    return pl.pallas_call(
        kernel,
        out_shape=outs,
        in_specs=[VMEM] * len(args),
        out_specs=jax.tree.map(lambda _: VMEM, outs),
        scratch_shapes=list(scratch),
        compiler_params=PARAMS,
    )(*args)


def load(ref, rows):
    return [[ref[i, j, rows, :] for j in range(F)] for i in range(F)]


def save(ref, rows, matrix):
    for i in range(F):
        for j in range(F):
            ref[i, j, rows, :] = matrix[i][j]


def total(terms):
    out = terms[0]
    for term in terms[1:]:
        out = lax.add(out, term)
    return out


def mul(left, right):
    return [
        [total([lax.mul(left[i][k], right[k][j]) for k in range(F)]) for j in range(F)]
        for i in range(F)
    ]


def mulvec(left, vector):
    return [total([lax.mul(left[i][k], vector[k]) for k in range(F)]) for i in range(F)]


def neg(matrix):
    return [[lax.neg(e) for e in row] for row in matrix]


def plus(*matrices):
    return [[total([m[i][j] for m in matrices]) for j in range(F)] for i in range(F)]


def invert(matrix):
    a = [list(row) for row in matrix]
    one = jnp.ones_like(a[0][0])
    for k in range(F):
        pivot = one / a[k][k]
        a[k] = [pivot if j == k else lax.mul(a[k][j], pivot) for j in range(F)]
        for i in range(F):
            if i != k:
                f = a[i][k]
                a[i] = [
                    lax.neg(lax.mul(f, pivot)) if j == k else lax.sub(a[i][j], lax.mul(f, a[k][j]))
                    for j in range(F)
                ]
    return a


def levels_of(count):
    sizes, base = [], 0
    while count > 8:
        half = count // 2
        sizes.append((half, base))
        base += 5 * half
        count = half
    return sizes, base


def factor_kernel(low, mid, high, out, *scratch):
    count = low.shape[2]
    sizes, base = levels_of(count)
    depth = len(sizes)
    lows, mids, highs = scratch[:depth], scratch[depth : 2 * depth], scratch[2 * depth : 3 * depth]
    inv_buf, low_pad, inv_pad, high_pad = scratch[3 * depth :]
    for source, target in ((low, lows[0]), (mid, mids[0]), (high, highs[0])):
        target[:, :, :count, :] = source[...]
    for group in (lows, mids, highs):
        for buf in group:
            rows = buf.shape[2]
            buf[:, :, rows - 8 :, :] = jnp.zeros((F, F, 8, buf.shape[3]), jnp.float32)
    for buf in (low_pad, inv_pad, high_pad):
        buf[...] = jnp.zeros_like(buf)
    last = None
    for level, (half, at) in enumerate(sizes):
        lo, mi, hi = lows[level], mids[level], highs[level]
        inv_buf[:, :, half : half + 8, :] = jnp.zeros((F, F, 8, inv_buf.shape[3]), jnp.float32)
        for c in range(half // 8):
            inv = invert(load(mi, pl.ds(16 * c, 8, 2)))
            save(inv_buf, pl.ds(8 * c, 8), inv)
            save(out, pl.ds(at + 8 * c, 8), inv)
        for c in range(half // 8):
            inv = load(inv_buf, pl.ds(8 * c, 8))
            low_even = load(lo, pl.ds(16 * c, 8, 2))
            high_even = load(hi, pl.ds(16 * c, 8, 2))
            alpha = neg(mul(load(lo, pl.ds(16 * c + 1, 8, 2)), inv))
            save(out, pl.ds(at + half + 8 * c, 8), alpha)
            save(out, pl.ds(at + 3 * half + 8 * c, 8), low_even)
            save(out, pl.ds(at + 4 * half + 8 * c, 8), high_even)
            low_new = mul(alpha, low_even)
            mid_part = plus(load(mi, pl.ds(16 * c + 1, 8, 2)), mul(alpha, high_even))
            gamma = neg(mul(load(hi, pl.ds(16 * c + 1, 8, 2)), load(inv_buf, pl.ds(8 * c + 1, 8))))
            save(out, pl.ds(at + 2 * half + 8 * c, 8), gamma)
            mid_new = plus(mid_part, mul(gamma, load(lo, pl.ds(16 * c + 2, 8, 2))))
            high_new = mul(gamma, load(hi, pl.ds(16 * c + 2, 8, 2)))
            if level + 1 < depth:
                save(lows[level + 1], pl.ds(8 * c, 8), low_new)
                save(mids[level + 1], pl.ds(8 * c, 8), mid_new)
                save(highs[level + 1], pl.ds(8 * c, 8), high_new)
            else:
                last = (low_new, mid_new, high_new)
    lo, mi, hi = last
    for index, step in enumerate((1, 2, 4)):
        save(low_pad, pl.ds(8, 8), lo)
        save(high_pad, pl.ds(8, 8), hi)
        save(inv_pad, pl.ds(8, 8), invert(mi))
        below, above = pl.ds(8 - step, 8), pl.ds(8 + step, 8)
        alpha = neg(mul(lo, load(inv_pad, below)))
        gamma = neg(mul(hi, load(inv_pad, above)))
        save(out, pl.ds(base + 16 * index, 8), alpha)
        save(out, pl.ds(base + 16 * index + 8, 8), gamma)
        mi = plus(mi, mul(alpha, load(high_pad, below)), mul(gamma, load(low_pad, above)))
        lo = mul(alpha, load(low_pad, below))
        hi = mul(gamma, load(high_pad, above))
    save(out, pl.ds(base + 48, 8), invert(mi))


def factor(low, mid, high):
    count, lanes = low.shape[2:]
    sizes, base = levels_of(count)
    pads = [pltpu.VMEM((F, F, 2 * half + 8, lanes), jnp.float32) for half, _ in sizes]
    scratch = pads * 3 + [pltpu.VMEM((F, F, count // 2 + 8, lanes), jnp.float32)]
    scratch += [pltpu.VMEM((F, F, 24, lanes), jnp.float32)] * 3
    out = jax.ShapeDtypeStruct((F, F, base + 56, lanes), jnp.float32)
    return call(factor_kernel, out, low, mid, high, scratch=scratch)


def vload(ref, rows):
    return [ref[i, rows, :] for i in range(F)]


def vsave(ref, rows, vector):
    for i in range(F):
        ref[i, rows, :] = vector[i]


def vplus(*vectors):
    return [total([v[i] for v in vectors]) for i in range(F)]


def vminus(a, b):
    return [lax.sub(x, y) for x, y in zip(a, b)]


def solve_kernel(fac, given, out, *scratch):
    parts, rows, lanes = given.shape
    piece = rows // F
    sizes, base = levels_of(parts * piece)
    depth = len(sizes)
    vals, sols = scratch[:depth], scratch[depth : 2 * depth]
    pad, top = scratch[2 * depth :]
    for f in range(F):
        for s in range(parts):
            vals[0][f, s * piece : (s + 1) * piece, :] = given[s, f * piece : (f + 1) * piece, :]
    for buf in vals:
        buf[:, buf.shape[1] - 8 :, :] = jnp.zeros((F, 8, lanes), jnp.float32)
    for buf in tuple(sols) + (top,):
        buf[:, :8, :] = jnp.zeros((F, 8, lanes), jnp.float32)
    pad[...] = jnp.zeros_like(pad)
    value = None
    for level, (half, at) in enumerate(sizes):
        val = vals[level]
        for c in range(half // 8):
            value = vplus(
                vload(val, pl.ds(16 * c + 1, 8, 2)),
                mulvec(load(fac, pl.ds(at + half + 8 * c, 8)), vload(val, pl.ds(16 * c, 8, 2))),
                mulvec(load(fac, pl.ds(at + 2 * half + 8 * c, 8)), vload(val, pl.ds(16 * c + 2, 8, 2))),
            )
            if level + 1 < depth:
                vsave(vals[level + 1], pl.ds(8 * c, 8), value)
    for index, step in enumerate((1, 2, 4)):
        vsave(pad, pl.ds(8, 8), value)
        value = vplus(
            value,
            mulvec(load(fac, pl.ds(base + 16 * index, 8)), vload(pad, pl.ds(8 - step, 8))),
            mulvec(load(fac, pl.ds(base + 16 * index + 8, 8)), vload(pad, pl.ds(8 + step, 8))),
        )
    vsave(top, pl.ds(8, 8), mulvec(load(fac, pl.ds(base + 48, 8)), value))
    above = top
    for level in reversed(range(depth)):
        half, at = sizes[level]
        for c in range(half // 8):
            x_odd = vload(above, pl.ds(8 + 8 * c, 8))
            x_prev = vload(above, pl.ds(7 + 8 * c, 8))
            rest = vminus(
                vminus(
                    vload(vals[level], pl.ds(16 * c, 8, 2)),
                    mulvec(load(fac, pl.ds(at + 3 * half + 8 * c, 8)), x_prev),
                ),
                mulvec(load(fac, pl.ds(at + 4 * half + 8 * c, 8)), x_odd),
            )
            x_even = mulvec(load(fac, pl.ds(at + 8 * c, 8)), rest)
            vsave(sols[level], pl.ds(8 + 16 * c, 8, 2), x_even)
            vsave(sols[level], pl.ds(9 + 16 * c, 8, 2), x_odd)
        above = sols[level]
    for f in range(F):
        for s in range(parts):
            out[s, f * piece : (f + 1) * piece, :] = above[f, 8 + s * piece : 8 + (s + 1) * piece, :]


def solve(fac, given):
    parts, rows, lanes = given.shape
    sizes, _ = levels_of(parts * rows // F)
    pads = [pltpu.VMEM((F, 2 * half + 8, lanes), jnp.float32) for half, _ in sizes]
    scratch = pads * 2 + [pltpu.VMEM((F, 24, lanes), jnp.float32), pltpu.VMEM((F, 16, lanes), jnp.float32)]
    return call(solve_kernel, jax.ShapeDtypeStruct(given.shape, jnp.float32), fac, given, scratch=scratch)


def each(count, step):
    if count <= 8:
        for d in range(count):
            step(d)
    else:

        @pl.loop(0, count)
        def _(d):
            step(d)


def place_hot(places, cap, d):
    shape = (cap, places.shape[1])
    at = lax.broadcasted_iota(jnp.int32, shape, 0) + d * cap
    return (at == jnp.broadcast_to(places, shape)).astype(jnp.float32)


def line_hot(row, line_dev):
    shape = (line_dev, row.shape[1])
    at = lax.broadcasted_iota(jnp.int32, shape, 0)
    return (at == jnp.broadcast_to(row, shape)).astype(jnp.float32)


def pack_first_kernel(cap, rhs, owner_row, owner_col, within, places_out, out):
    slots = rhs.shape[1]
    shape = (slots, slots)
    row = jnp.broadcast_to(owner_row[...], shape)
    same = row == jnp.broadcast_to(owner_col[...], shape)
    before = lax.broadcasted_iota(jnp.int32, shape, 0) < lax.broadcasted_iota(jnp.int32, shape, 1)
    rank = jnp.sum((same & before).astype(jnp.float32), axis=0, keepdims=True).astype(jnp.int32)
    places = owner_row[...] * cap + rank
    places_out[...] = places
    tags = jnp.broadcast_to((within[...] + 1).astype(jnp.float32), (8, slots))
    full = jnp.concatenate([rhs[...], tags], axis=0)

    def step(d):
        out[d] = dot(full, place_hot(places_out[...], cap, d), NT)

    each(out.shape[0], step)


def pack_second_kernel(cap, rhs, lateral, first, low, high, places, out):
    rows, slots = rhs.shape
    lane = lax.broadcasted_iota(jnp.int32, (rows, slots), 1)
    here = first[...]
    below = jnp.where(lane == 0, jnp.broadcast_to(low[...], here.shape), pltpu.roll(here, 1, 1))
    above = jnp.where(
        lane == slots - 1, jnp.broadcast_to(high[...], here.shape), pltpu.roll(here, slots - 1, 1)
    )
    residual = rhs[...] + lateral[...] * (below + above)

    def step(d):
        out[d] = dot(residual, place_hot(places[...], cap, d), NT)

    each(out.shape[0], step)


def arrive_kernel(received, arrived, out, acc):
    acc[...] = jnp.zeros_like(acc)
    rows, line_dev = acc.shape

    def step(d):
        acc[...] += dot(received[d, :rows, :], line_hot(arrived[d], line_dev), NT)

    each(received.shape[0], step)
    quarter = out.shape[2]
    for q in range(out.shape[0]):
        out[q] = acc[:, q * quarter : (q + 1) * quarter]


def reply_kernel(returned, arrived, out):
    lines = jnp.concatenate([returned[q] for q in range(returned.shape[0])], axis=1)

    def step(d):
        out[d] = dot(lines, line_hot(arrived[d], lines.shape[1]), NN)

    each(out.shape[0], step)


def home_kernel(home, places, out):
    out[...] = jnp.zeros_like(out)
    cap = home.shape[2]

    def step(d):
        out[...] += dot(home[d], place_hot(places[...], cap, d), NN)

    each(home.shape[0], step)


def exchange(buffer, axis):
    return lax.all_to_all(buffer, axis, split_axis=0, concat_axis=0, tiled=True)


def body(rhs, lateral, piece_line, lower, diag_blocks, upper):
    fields, piece, line_dev = rhs.shape
    n_dom, n_sub = lax.axis_size("dom"), lax.axis_size("sub")
    mean_load = line_dev // n_dom
    cap = mean_load + (mean_load + 1) // 2
    rows = fields * piece
    f32 = lambda *shape: jax.ShapeDtypeStruct(shape, jnp.float32)
    rhs = rhs.reshape(rows, line_dev)
    lateral = lateral.reshape(rows, line_dev)
    owners = piece_line // line_dev
    within = piece_line % line_dev
    places, buffer = call(
        functools.partial(pack_first_kernel, cap),
        [jax.ShapeDtypeStruct((1, line_dev), jnp.int32), f32(n_dom, rows + 8, cap)],
        rhs, owners, owners.reshape(line_dev, 1), within,
    )
    received = exchange(buffer, "dom")
    fac = factor(lower, diag_blocks, upper)
    arrived = received[:, rows : rows + 1, :].astype(jnp.int32) - 1

    def finish(received):
        quarters = call(
            arrive_kernel, f32(n_sub, rows, line_dev // n_sub), received, arrived,
            scratch=[pltpu.VMEM((rows, line_dev), jnp.float32)],
        )
        solved = solve(fac, exchange(quarters, "sub"))
        reply = call(reply_kernel, f32(n_dom, rows, cap), exchange(solved, "sub"), arrived)
        return call(home_kernel, f32(rows, line_dev), exchange(reply, "dom"), places)

    first = finish(received)
    forward = [(i, i + 1) for i in range(n_dom - 1)]
    backward = [(b, a) for a, b in forward]
    low = lax.ppermute(first[:, line_dev - 1 :], "dom", forward)
    high = lax.ppermute(first[:, :1], "dom", backward)
    second = call(
        functools.partial(pack_second_kernel, cap), f32(n_dom, rows, cap),
        rhs, lateral, first, low, high, places,
    )
    return finish(exchange(second, "dom")).reshape(fields, piece, line_dev)


def solution(mesh):
    placed = (
        P(None, "sub", "dom"),
        P(None, "sub", "dom"),
        P("sub", "dom"),
        P(None, None, None, ("dom", "sub")),
        P(None, None, None, ("dom", "sub")),
        P(None, None, None, ("dom", "sub")),
    )
    return jax.shard_map(
        body, mesh=mesh, in_specs=placed, out_specs=P(None, "sub", "dom"), check_vma=False
    )
```

```python
import functools

import jax
import jax.numpy as jnp
from jax import lax
from jax.experimental import pallas as pl
from jax.experimental.pallas import tpu as pltpu
from jax.sharding import PartitionSpec as P

F = 5
VMEM = pl.BlockSpec(memory_space=pltpu.VMEM)
PARAMS = pltpu.CompilerParams(vmem_limit_bytes=40 * 1024 * 1024)
NT = (((1,), (1,)), ((), ()))
NN = (((1,), (0,)), ((), ()))
MESH = pl.DeviceIdType.MESH


def dot(left, right, dims):
    return lax.dot_general(
        left, right, dims, precision=lax.Precision.HIGHEST, preferred_element_type=jnp.float32
    )


def call(kernel, outs, *args, scratch=(), params=PARAMS):
    return pl.pallas_call(
        kernel,
        out_shape=outs,
        in_specs=[VMEM] * len(args),
        out_specs=jax.tree.map(lambda _: VMEM, outs),
        scratch_shapes=list(scratch),
        compiler_params=params,
    )(*args)


def load(ref, rows):
    return [[ref[i, j, rows, :] for j in range(F)] for i in range(F)]


def save(ref, rows, matrix):
    for i in range(F):
        for j in range(F):
            ref[i, j, rows, :] = matrix[i][j]


def total(terms):
    out = terms[0]
    for term in terms[1:]:
        out = lax.add(out, term)
    return out


def mul(left, right):
    return [
        [total([lax.mul(left[i][k], right[k][j]) for k in range(F)]) for j in range(F)]
        for i in range(F)
    ]


def mulvec(left, vector):
    return [total([lax.mul(left[i][k], vector[k]) for k in range(F)]) for i in range(F)]


def neg(matrix):
    return [[lax.neg(e) for e in row] for row in matrix]


def plus(*matrices):
    return [[total([m[i][j] for m in matrices]) for j in range(F)] for i in range(F)]


def invert(matrix):
    a = [list(row) for row in matrix]
    one = jnp.ones_like(a[0][0])
    for k in range(F):
        pivot = one / a[k][k]
        a[k] = [pivot if j == k else lax.mul(a[k][j], pivot) for j in range(F)]
        for i in range(F):
            if i != k:
                f = a[i][k]
                a[i] = [
                    lax.neg(lax.mul(f, pivot)) if j == k else lax.sub(a[i][j], lax.mul(f, a[k][j]))
                    for j in range(F)
                ]
    return a


def levels_of(count):
    sizes, base = [], 0
    while count > 8:
        half = count // 2
        sizes.append((half, base))
        base += 5 * half
        count = half
    return sizes, base


def factor_kernel(low, mid, high, out, *scratch):
    count = low.shape[2]
    sizes, base = levels_of(count)
    depth = len(sizes)
    lows, mids, highs = scratch[:depth], scratch[depth : 2 * depth], scratch[2 * depth : 3 * depth]
    inv_buf, low_pad, inv_pad, high_pad = scratch[3 * depth :]
    for source, target in ((low, lows[0]), (mid, mids[0]), (high, highs[0])):
        target[:, :, :count, :] = source[...]
    for group in (lows, mids, highs):
        for buf in group:
            rows = buf.shape[2]
            buf[:, :, rows - 8 :, :] = jnp.zeros((F, F, 8, buf.shape[3]), jnp.float32)
    for buf in (low_pad, inv_pad, high_pad):
        buf[...] = jnp.zeros_like(buf)
    last = None
    for level, (half, at) in enumerate(sizes):
        lo, mi, hi = lows[level], mids[level], highs[level]
        inv_buf[:, :, half : half + 8, :] = jnp.zeros((F, F, 8, inv_buf.shape[3]), jnp.float32)
        for c in range(half // 8):
            inv = invert(load(mi, pl.ds(16 * c, 8, 2)))
            save(inv_buf, pl.ds(8 * c, 8), inv)
            save(out, pl.ds(at + 8 * c, 8), inv)
        for c in range(half // 8):
            inv = load(inv_buf, pl.ds(8 * c, 8))
            low_even = load(lo, pl.ds(16 * c, 8, 2))
            high_even = load(hi, pl.ds(16 * c, 8, 2))
            alpha = neg(mul(load(lo, pl.ds(16 * c + 1, 8, 2)), inv))
            save(out, pl.ds(at + half + 8 * c, 8), alpha)
            save(out, pl.ds(at + 3 * half + 8 * c, 8), low_even)
            save(out, pl.ds(at + 4 * half + 8 * c, 8), high_even)
            low_new = mul(alpha, low_even)
            mid_part = plus(load(mi, pl.ds(16 * c + 1, 8, 2)), mul(alpha, high_even))
            gamma = neg(mul(load(hi, pl.ds(16 * c + 1, 8, 2)), load(inv_buf, pl.ds(8 * c + 1, 8))))
            save(out, pl.ds(at + 2 * half + 8 * c, 8), gamma)
            mid_new = plus(mid_part, mul(gamma, load(lo, pl.ds(16 * c + 2, 8, 2))))
            high_new = mul(gamma, load(hi, pl.ds(16 * c + 2, 8, 2)))
            if level + 1 < depth:
                save(lows[level + 1], pl.ds(8 * c, 8), low_new)
                save(mids[level + 1], pl.ds(8 * c, 8), mid_new)
                save(highs[level + 1], pl.ds(8 * c, 8), high_new)
            else:
                last = (low_new, mid_new, high_new)
    lo, mi, hi = last
    for index, step in enumerate((1, 2, 4)):
        save(low_pad, pl.ds(8, 8), lo)
        save(high_pad, pl.ds(8, 8), hi)
        save(inv_pad, pl.ds(8, 8), invert(mi))
        below, above = pl.ds(8 - step, 8), pl.ds(8 + step, 8)
        alpha = neg(mul(lo, load(inv_pad, below)))
        gamma = neg(mul(hi, load(inv_pad, above)))
        save(out, pl.ds(base + 16 * index, 8), alpha)
        save(out, pl.ds(base + 16 * index + 8, 8), gamma)
        mi = plus(mi, mul(alpha, load(high_pad, below)), mul(gamma, load(low_pad, above)))
        lo = mul(alpha, load(low_pad, below))
        hi = mul(gamma, load(high_pad, above))
    save(out, pl.ds(base + 48, 8), invert(mi))


def factor(low, mid, high):
    count, lanes = low.shape[2:]
    sizes, base = levels_of(count)
    pads = [pltpu.VMEM((F, F, 2 * half + 8, lanes), jnp.float32) for half, _ in sizes]
    scratch = pads * 3 + [pltpu.VMEM((F, F, count // 2 + 8, lanes), jnp.float32)]
    scratch += [pltpu.VMEM((F, F, 24, lanes), jnp.float32)] * 3
    out = jax.ShapeDtypeStruct((F, F, base + 56, lanes), jnp.float32)
    return call(factor_kernel, out, low, mid, high, scratch=scratch)


def vload(ref, rows):
    return [ref[i, rows, :] for i in range(F)]


def vsave(ref, rows, vector):
    for i in range(F):
        ref[i, rows, :] = vector[i]


def vplus(*vectors):
    return [total([v[i] for v in vectors]) for i in range(F)]


def vminus(a, b):
    return [lax.sub(x, y) for x, y in zip(a, b)]


def solve_kernel(fac, given, out, *scratch):
    parts, rows, lanes = given.shape
    piece = rows // F
    sizes, base = levels_of(parts * piece)
    depth = len(sizes)
    vals, sols = scratch[:depth], scratch[depth : 2 * depth]
    pad, top = scratch[2 * depth :]
    for f in range(F):
        for s in range(parts):
            vals[0][f, s * piece : (s + 1) * piece, :] = given[s, f * piece : (f + 1) * piece, :]
    for buf in vals:
        buf[:, buf.shape[1] - 8 :, :] = jnp.zeros((F, 8, lanes), jnp.float32)
    for buf in tuple(sols) + (top,):
        buf[:, :8, :] = jnp.zeros((F, 8, lanes), jnp.float32)
    pad[...] = jnp.zeros_like(pad)
    value = None
    for level, (half, at) in enumerate(sizes):
        val = vals[level]
        for c in range(half // 8):
            value = vplus(
                vload(val, pl.ds(16 * c + 1, 8, 2)),
                mulvec(load(fac, pl.ds(at + half + 8 * c, 8)), vload(val, pl.ds(16 * c, 8, 2))),
                mulvec(load(fac, pl.ds(at + 2 * half + 8 * c, 8)), vload(val, pl.ds(16 * c + 2, 8, 2))),
            )
            if level + 1 < depth:
                vsave(vals[level + 1], pl.ds(8 * c, 8), value)
    for index, step in enumerate((1, 2, 4)):
        vsave(pad, pl.ds(8, 8), value)
        value = vplus(
            value,
            mulvec(load(fac, pl.ds(base + 16 * index, 8)), vload(pad, pl.ds(8 - step, 8))),
            mulvec(load(fac, pl.ds(base + 16 * index + 8, 8)), vload(pad, pl.ds(8 + step, 8))),
        )
    vsave(top, pl.ds(8, 8), mulvec(load(fac, pl.ds(base + 48, 8)), value))
    above = top
    for level in reversed(range(depth)):
        half, at = sizes[level]
        for c in range(half // 8):
            x_odd = vload(above, pl.ds(8 + 8 * c, 8))
            x_prev = vload(above, pl.ds(7 + 8 * c, 8))
            rest = vminus(
                vminus(
                    vload(vals[level], pl.ds(16 * c, 8, 2)),
                    mulvec(load(fac, pl.ds(at + 3 * half + 8 * c, 8)), x_prev),
                ),
                mulvec(load(fac, pl.ds(at + 4 * half + 8 * c, 8)), x_odd),
            )
            x_even = mulvec(load(fac, pl.ds(at + 8 * c, 8)), rest)
            vsave(sols[level], pl.ds(8 + 16 * c, 8, 2), x_even)
            vsave(sols[level], pl.ds(9 + 16 * c, 8, 2), x_odd)
        above = sols[level]
    for f in range(F):
        for s in range(parts):
            out[s, f * piece : (f + 1) * piece, :] = above[f, 8 + s * piece : 8 + (s + 1) * piece, :]


def solve(fac, given):
    parts, rows, lanes = given.shape
    sizes, _ = levels_of(parts * rows // F)
    pads = [pltpu.VMEM((F, 2 * half + 8, lanes), jnp.float32) for half, _ in sizes]
    scratch = pads * 2 + [pltpu.VMEM((F, 24, lanes), jnp.float32), pltpu.VMEM((F, 16, lanes), jnp.float32)]
    return call(solve_kernel, jax.ShapeDtypeStruct(given.shape, jnp.float32), fac, given, scratch=scratch)


def each(count, step):
    if count <= 8:
        for d in range(count):
            step(d)
    else:

        @pl.loop(0, count)
        def _(d):
            step(d)


def place_hot(places, cap, d):
    shape = (cap, places.shape[1])
    at = lax.broadcasted_iota(jnp.int32, shape, 0) + d * cap
    return (at == jnp.broadcast_to(places, shape)).astype(jnp.float32)


def line_hot(row, line_dev):
    shape = (line_dev, row.shape[1])
    at = lax.broadcasted_iota(jnp.int32, shape, 0)
    return (at == jnp.broadcast_to(row, shape)).astype(jnp.float32)


def pack_first_kernel(cap, rhs, owner_row, owner_col, within, places_out, out):
    slots = rhs.shape[1]
    shape = (slots, slots)
    row = jnp.broadcast_to(owner_row[...], shape)
    same = row == jnp.broadcast_to(owner_col[...], shape)
    before = lax.broadcasted_iota(jnp.int32, shape, 0) < lax.broadcasted_iota(jnp.int32, shape, 1)
    rank = jnp.sum((same & before).astype(jnp.float32), axis=0, keepdims=True).astype(jnp.int32)
    places = owner_row[...] * cap + rank
    places_out[...] = places
    tags = jnp.broadcast_to((within[...] + 1).astype(jnp.float32), (8, slots))
    full = jnp.concatenate([rhs[...], tags], axis=0)

    def step(d):
        out[d] = dot(full, place_hot(places_out[...], cap, d), NT)

    each(out.shape[0], step)


def pack_second_kernel(cap, rhs, lateral, first, places, out, low_edge, high_edge, send, recv):
    rows, slots = rhs.shape
    count = lax.axis_size("dom")
    me = lax.axis_index("dom")
    right, left = lax.rem(me + 1, count), lax.rem(me + count - 1, count)
    greet("dom", [right, left])
    copies = [
        pltpu.make_async_remote_copy(
            src_ref=first.at[:, pl.ds(start, 128)], dst_ref=edge, send_sem=send.at[i],
            recv_sem=recv.at[i], device_id={"dom": other}, device_id_type=MESH,
        )
        for i, (start, edge, other) in enumerate(
            ((slots - 128, low_edge, right), (0, high_edge, left))
        )
    ]
    for copy in copies:
        copy.start()
    for copy in copies:
        copy.wait()
    low = jnp.where(me == 0, 0.0, low_edge[:, 127:128])
    high = jnp.where(me == count - 1, 0.0, high_edge[:, 0:1])
    lane = lax.broadcasted_iota(jnp.int32, (rows, slots), 1)
    here = first[...]
    below = jnp.where(lane == 0, jnp.broadcast_to(low, here.shape), pltpu.roll(here, 1, 1))
    above = jnp.where(
        lane == slots - 1, jnp.broadcast_to(high, here.shape), pltpu.roll(here, slots - 1, 1)
    )
    residual = rhs[...] + lateral[...] * (below + above)

    def step(d):
        out[d] = dot(residual, place_hot(places[...], cap, d), NT)

    each(out.shape[0], step)


def arrive_kernel(received, arrived, out, acc):
    acc[...] = jnp.zeros_like(acc)
    rows, line_dev = acc.shape

    def step(d):
        acc[...] += dot(received[d, :rows, :], line_hot(arrived[d], line_dev), NT)

    each(received.shape[0], step)
    quarter = out.shape[2]
    for q in range(out.shape[0]):
        out[q] = acc[:, q * quarter : (q + 1) * quarter]


def reply_kernel(returned, arrived, out):
    lines = jnp.concatenate([returned[q] for q in range(returned.shape[0])], axis=1)

    def step(d):
        out[d] = dot(lines, line_hot(arrived[d], lines.shape[1]), NN)

    each(out.shape[0], step)


def home_kernel(home, places, out):
    out[...] = jnp.zeros_like(out)
    cap = home.shape[2]

    def step(d):
        out[...] += dot(home[d], place_hot(places[...], cap, d), NN)

    each(home.shape[0], step)


def greet(axis, others):
    barrier = pltpu.get_barrier_semaphore()
    for other in others:
        pl.semaphore_signal(barrier, inc=1, device_id={axis: other}, device_id_type=MESH)
    pl.semaphore_wait(barrier, len(others))


def exchange_kernel(axis, given, out, send, recv, own):
    count = given.shape[0]
    me = lax.axis_index(axis)
    keep = pltpu.make_async_copy(given.at[me], out.at[me], own)
    keep.start()
    greet(axis, [lax.rem(me + i, count) for i in range(1, count)])

    def copy(i, source, target, other):
        return pltpu.make_async_remote_copy(
            src_ref=given.at[source], dst_ref=out.at[target], send_sem=send.at[i],
            recv_sem=recv.at[i], device_id={axis: other}, device_id_type=MESH,
        )

    for i in range(1, count):
        other = lax.rem(me + i, count)
        copy(i, other, me, other).start()
    for i in range(1, count):
        other = lax.rem(me + count - i, count)
        copy(i, other, other, other).wait_recv()
    for i in range(1, count):
        other = lax.rem(me + i, count)
        copy(i, other, me, other).wait_send()
    keep.wait()


def exchange(buffer, axis, number):
    count = buffer.shape[0]
    return pl.pallas_call(
        functools.partial(exchange_kernel, axis),
        out_shape=jax.ShapeDtypeStruct(buffer.shape, buffer.dtype),
        in_specs=[VMEM],
        out_specs=VMEM,
        scratch_shapes=[
            pltpu.SemaphoreType.DMA((count,)), pltpu.SemaphoreType.DMA((count,)), pltpu.SemaphoreType.DMA,
        ],
        compiler_params=pltpu.CompilerParams(
            vmem_limit_bytes=40 * 1024 * 1024, collective_id=number, has_side_effects=True
        ),
    )(buffer)


def body(rhs, lateral, piece_line, lower, diag_blocks, upper):
    fields, piece, line_dev = rhs.shape
    n_dom, n_sub = lax.axis_size("dom"), lax.axis_size("sub")
    mean_load = line_dev // n_dom
    cap = mean_load + (mean_load + 1) // 2
    rows = fields * piece
    f32 = lambda *shape: jax.ShapeDtypeStruct(shape, jnp.float32)
    rhs = rhs.reshape(rows, line_dev)
    lateral = lateral.reshape(rows, line_dev)
    owners = piece_line // line_dev
    within = piece_line % line_dev
    places, buffer = call(
        functools.partial(pack_first_kernel, cap),
        [jax.ShapeDtypeStruct((1, line_dev), jnp.int32), f32(n_dom, rows + 8, cap)],
        rhs, owners, owners.reshape(line_dev, 1), within,
    )
    received = exchange(buffer, "dom", 0)
    fac = factor(lower, diag_blocks, upper)
    arrived = received[:, rows : rows + 1, :].astype(jnp.int32) - 1

    def finish(received):
        quarters = call(
            arrive_kernel, f32(n_sub, rows, line_dev // n_sub), received, arrived,
            scratch=[pltpu.VMEM((rows, line_dev), jnp.float32)],
        )
        solved = solve(fac, exchange(quarters, "sub", 2))
        reply = call(reply_kernel, f32(n_dom, rows, cap), exchange(solved, "sub", 2), arrived)
        return call(home_kernel, f32(rows, line_dev), exchange(reply, "dom", 1), places)

    first = finish(received)
    second = call(
        functools.partial(pack_second_kernel, cap), f32(n_dom, rows, cap),
        rhs, lateral, first, places,
        scratch=[pltpu.VMEM((rows, 128), jnp.float32)] * 2 + [pltpu.SemaphoreType.DMA((2,))] * 2,
        params=pltpu.CompilerParams(
            vmem_limit_bytes=40 * 1024 * 1024, collective_id=3, has_side_effects=True
        ),
    )
    return finish(exchange(second, "dom", 1)).reshape(fields, piece, line_dev)


def solution(mesh):
    placed = (
        P(None, "sub", "dom"),
        P(None, "sub", "dom"),
        P("sub", "dom"),
        P(None, None, None, ("dom", "sub")),
        P(None, None, None, ("dom", "sub")),
        P(None, None, None, ("dom", "sub")),
    )
    return jax.shard_map(
        body, mesh=mesh, in_specs=placed, out_specs=P(None, "sub", "dom"), check_vma=False
    )
```

```python
import functools

import jax
import jax.numpy as jnp
from jax import lax
from jax.experimental import pallas as pl
from jax.experimental.pallas import tpu as pltpu
from jax.sharding import PartitionSpec as P

F = 5
VMEM = pl.BlockSpec(memory_space=pltpu.VMEM)
PARAMS = pltpu.CompilerParams(vmem_limit_bytes=40 * 1024 * 1024)
NT = (((1,), (1,)), ((), ()))
NN = (((1,), (0,)), ((), ()))
MESH = pl.DeviceIdType.MESH


def dot(left, right, dims):
    return lax.dot_general(
        left, right, dims, precision=lax.Precision.HIGHEST, preferred_element_type=jnp.float32
    )


def call(kernel, outs, *args, scratch=(), params=PARAMS, space=VMEM):
    return pl.pallas_call(
        kernel,
        out_shape=outs,
        in_specs=[space] * len(args),
        out_specs=jax.tree.map(lambda _: VMEM, outs),
        scratch_shapes=list(scratch),
        compiler_params=params,
    )(*args)


def load(ref, rows):
    return [[ref[i, j, rows, :] for j in range(F)] for i in range(F)]


def save(ref, rows, matrix):
    for i in range(F):
        for j in range(F):
            ref[i, j, rows, :] = matrix[i][j]


def total(terms):
    out = terms[0]
    for term in terms[1:]:
        out = lax.add(out, term)
    return out


def mul(left, right):
    return [
        [total([lax.mul(left[i][k], right[k][j]) for k in range(F)]) for j in range(F)]
        for i in range(F)
    ]


def mulvec(left, vector):
    return [total([lax.mul(left[i][k], vector[k]) for k in range(F)]) for i in range(F)]


def neg(matrix):
    return [[lax.neg(e) for e in row] for row in matrix]


def plus(*matrices):
    return [[total([m[i][j] for m in matrices]) for j in range(F)] for i in range(F)]


def invert(matrix):
    a = [list(row) for row in matrix]
    one = jnp.ones_like(a[0][0])
    for k in range(F):
        pivot = one / a[k][k]
        a[k] = [pivot if j == k else lax.mul(a[k][j], pivot) for j in range(F)]
        for i in range(F):
            if i != k:
                f = a[i][k]
                a[i] = [
                    lax.neg(lax.mul(f, pivot)) if j == k else lax.sub(a[i][j], lax.mul(f, a[k][j]))
                    for j in range(F)
                ]
    return a


def levels_of(count):
    sizes, base = [], 0
    while count > 8:
        half = count // 2
        sizes.append((half, base))
        base += 5 * half
        count = half
    return sizes, base


def factor_kernel(low, mid, high, out, *scratch):
    count = low.shape[2]
    sizes, base = levels_of(count)
    depth = len(sizes)
    lows, mids, highs = scratch[:depth], scratch[depth : 2 * depth], scratch[2 * depth : 3 * depth]
    inv_buf, low_pad, inv_pad, high_pad, loaded = scratch[3 * depth :]
    loads = [
        pltpu.make_async_copy(source.at[i], target.at[i, :, pl.ds(0, count), :], loaded.at[n * F + i])
        for n, (source, target) in enumerate(((low, lows[0]), (mid, mids[0]), (high, highs[0])))
        for i in range(F)
    ]
    for copy in loads:
        copy.start()
    for group in (lows, mids, highs):
        for buf in group:
            rows = buf.shape[2]
            buf[:, :, rows - 8 :, :] = jnp.zeros((F, F, 8, buf.shape[3]), jnp.float32)
    for buf in (low_pad, inv_pad, high_pad):
        buf[...] = jnp.zeros_like(buf)
    for copy in loads:
        copy.wait()
    last = None
    for level, (half, at) in enumerate(sizes):
        lo, mi, hi = lows[level], mids[level], highs[level]
        inv_buf[:, :, half : half + 8, :] = jnp.zeros((F, F, 8, inv_buf.shape[3]), jnp.float32)
        for c in range(half // 8):
            inv = invert(load(mi, pl.ds(16 * c, 8, 2)))
            save(inv_buf, pl.ds(8 * c, 8), inv)
            save(out, pl.ds(at + 8 * c, 8), inv)
        for c in range(half // 8):
            inv = load(inv_buf, pl.ds(8 * c, 8))
            low_even = load(lo, pl.ds(16 * c, 8, 2))
            high_even = load(hi, pl.ds(16 * c, 8, 2))
            alpha = neg(mul(load(lo, pl.ds(16 * c + 1, 8, 2)), inv))
            save(out, pl.ds(at + half + 8 * c, 8), alpha)
            save(out, pl.ds(at + 3 * half + 8 * c, 8), low_even)
            save(out, pl.ds(at + 4 * half + 8 * c, 8), high_even)
            low_new = mul(alpha, low_even)
            mid_part = plus(load(mi, pl.ds(16 * c + 1, 8, 2)), mul(alpha, high_even))
            gamma = neg(mul(load(hi, pl.ds(16 * c + 1, 8, 2)), load(inv_buf, pl.ds(8 * c + 1, 8))))
            save(out, pl.ds(at + 2 * half + 8 * c, 8), gamma)
            mid_new = plus(mid_part, mul(gamma, load(lo, pl.ds(16 * c + 2, 8, 2))))
            high_new = mul(gamma, load(hi, pl.ds(16 * c + 2, 8, 2)))
            if level + 1 < depth:
                save(lows[level + 1], pl.ds(8 * c, 8), low_new)
                save(mids[level + 1], pl.ds(8 * c, 8), mid_new)
                save(highs[level + 1], pl.ds(8 * c, 8), high_new)
            else:
                last = (low_new, mid_new, high_new)
    lo, mi, hi = last
    for index, step in enumerate((1, 2, 4)):
        save(low_pad, pl.ds(8, 8), lo)
        save(high_pad, pl.ds(8, 8), hi)
        save(inv_pad, pl.ds(8, 8), invert(mi))
        below, above = pl.ds(8 - step, 8), pl.ds(8 + step, 8)
        alpha = neg(mul(lo, load(inv_pad, below)))
        gamma = neg(mul(hi, load(inv_pad, above)))
        save(out, pl.ds(base + 16 * index, 8), alpha)
        save(out, pl.ds(base + 16 * index + 8, 8), gamma)
        mi = plus(mi, mul(alpha, load(high_pad, below)), mul(gamma, load(low_pad, above)))
        lo = mul(alpha, load(low_pad, below))
        hi = mul(gamma, load(high_pad, above))
    save(out, pl.ds(base + 48, 8), invert(mi))


def factor(low, mid, high):
    count, lanes = low.shape[2:]
    sizes, base = levels_of(count)
    pads = [pltpu.VMEM((F, F, 2 * half + 8, lanes), jnp.float32) for half, _ in sizes]
    scratch = pads * 3 + [pltpu.VMEM((F, F, count // 2 + 8, lanes), jnp.float32)]
    scratch += [pltpu.VMEM((F, F, 24, lanes), jnp.float32)] * 3 + [pltpu.SemaphoreType.DMA((3 * F,))]
    out = jax.ShapeDtypeStruct((F, F, base + 56, lanes), jnp.float32)
    return call(factor_kernel, out, low, mid, high, scratch=scratch, space=pl.BlockSpec(memory_space=pltpu.HBM))


def vload(ref, rows):
    return [ref[i, rows, :] for i in range(F)]


def vsave(ref, rows, vector):
    for i in range(F):
        ref[i, rows, :] = vector[i]


def vplus(*vectors):
    return [total([v[i] for v in vectors]) for i in range(F)]


def vminus(a, b):
    return [lax.sub(x, y) for x, y in zip(a, b)]


def solve_kernel(fac, given, out, *scratch):
    parts, rows, lanes = given.shape
    piece = rows // F
    sizes, base = levels_of(parts * piece)
    depth = len(sizes)
    vals, sols = scratch[:depth], scratch[depth : 2 * depth]
    pad, top = scratch[2 * depth :]
    for f in range(F):
        for s in range(parts):
            vals[0][f, s * piece : (s + 1) * piece, :] = given[s, f * piece : (f + 1) * piece, :]
    for buf in vals:
        buf[:, buf.shape[1] - 8 :, :] = jnp.zeros((F, 8, lanes), jnp.float32)
    for buf in tuple(sols) + (top,):
        buf[:, :8, :] = jnp.zeros((F, 8, lanes), jnp.float32)
    pad[...] = jnp.zeros_like(pad)
    value = None
    for level, (half, at) in enumerate(sizes):
        val = vals[level]
        for c in range(half // 8):
            value = vplus(
                vload(val, pl.ds(16 * c + 1, 8, 2)),
                mulvec(load(fac, pl.ds(at + half + 8 * c, 8)), vload(val, pl.ds(16 * c, 8, 2))),
                mulvec(load(fac, pl.ds(at + 2 * half + 8 * c, 8)), vload(val, pl.ds(16 * c + 2, 8, 2))),
            )
            if level + 1 < depth:
                vsave(vals[level + 1], pl.ds(8 * c, 8), value)
    for index, step in enumerate((1, 2, 4)):
        vsave(pad, pl.ds(8, 8), value)
        value = vplus(
            value,
            mulvec(load(fac, pl.ds(base + 16 * index, 8)), vload(pad, pl.ds(8 - step, 8))),
            mulvec(load(fac, pl.ds(base + 16 * index + 8, 8)), vload(pad, pl.ds(8 + step, 8))),
        )
    vsave(top, pl.ds(8, 8), mulvec(load(fac, pl.ds(base + 48, 8)), value))
    above = top
    for level in reversed(range(depth)):
        half, at = sizes[level]
        for c in range(half // 8):
            x_odd = vload(above, pl.ds(8 + 8 * c, 8))
            x_prev = vload(above, pl.ds(7 + 8 * c, 8))
            rest = vminus(
                vminus(
                    vload(vals[level], pl.ds(16 * c, 8, 2)),
                    mulvec(load(fac, pl.ds(at + 3 * half + 8 * c, 8)), x_prev),
                ),
                mulvec(load(fac, pl.ds(at + 4 * half + 8 * c, 8)), x_odd),
            )
            x_even = mulvec(load(fac, pl.ds(at + 8 * c, 8)), rest)
            vsave(sols[level], pl.ds(8 + 16 * c, 8, 2), x_even)
            vsave(sols[level], pl.ds(9 + 16 * c, 8, 2), x_odd)
        above = sols[level]
    for f in range(F):
        for s in range(parts):
            out[s, f * piece : (f + 1) * piece, :] = above[f, 8 + s * piece : 8 + (s + 1) * piece, :]


def solve(fac, given):
    parts, rows, lanes = given.shape
    sizes, _ = levels_of(parts * rows // F)
    pads = [pltpu.VMEM((F, 2 * half + 8, lanes), jnp.float32) for half, _ in sizes]
    scratch = pads * 2 + [pltpu.VMEM((F, 24, lanes), jnp.float32), pltpu.VMEM((F, 16, lanes), jnp.float32)]
    return call(solve_kernel, jax.ShapeDtypeStruct(given.shape, jnp.float32), fac, given, scratch=scratch)


def each(first, count, step):
    if count <= 8:
        for i in range(first, count):
            step(i)
    else:

        @pl.loop(first, count)
        def _(i):
            step(i)


def place_hot(places, cap, d):
    shape = (cap, places.shape[1])
    at = lax.broadcasted_iota(jnp.int32, shape, 0) + d * cap
    return (at == jnp.broadcast_to(places, shape)).astype(jnp.float32)


def line_hot(row, line_dev):
    shape = (line_dev, row.shape[1])
    at = lax.broadcasted_iota(jnp.int32, shape, 0)
    return (at == jnp.broadcast_to(row, shape)).astype(jnp.float32)


def greet(axis, others):
    barrier = pltpu.get_barrier_semaphore()
    for other in others:
        pl.semaphore_signal(barrier, inc=1, device_id={axis: other}, device_id_type=MESH)
    pl.semaphore_wait(barrier, len(others))


def exchange_kernel(axis, given, out, send, recv, own):
    count = given.shape[0]
    me = lax.axis_index(axis)
    keep = pltpu.make_async_copy(given.at[me], out.at[me], own)
    keep.start()
    greet(axis, [lax.rem(me + i, count) for i in range(1, count)])

    def copy(i, source, target, other):
        return pltpu.make_async_remote_copy(
            src_ref=given.at[source], dst_ref=out.at[target], send_sem=send.at[i],
            recv_sem=recv.at[i], device_id={axis: other}, device_id_type=MESH,
        )

    for i in range(1, count):
        other = lax.rem(me + i, count)
        copy(i, other, me, other).start()
    for i in range(1, count):
        other = lax.rem(me + count - i, count)
        copy(i, other, other, other).wait_recv()
    for i in range(1, count):
        other = lax.rem(me + i, count)
        copy(i, other, me, other).wait_send()
    keep.wait()


def exchange(buffer, axis, number):
    count = buffer.shape[0]
    return pl.pallas_call(
        functools.partial(exchange_kernel, axis),
        out_shape=jax.ShapeDtypeStruct(buffer.shape, buffer.dtype),
        in_specs=[VMEM],
        out_specs=VMEM,
        scratch_shapes=[
            pltpu.SemaphoreType.DMA((count,)), pltpu.SemaphoreType.DMA((count,)), pltpu.SemaphoreType.DMA,
        ],
        compiler_params=pltpu.CompilerParams(
            vmem_limit_bytes=40 * 1024 * 1024, collective_id=number, has_side_effects=True
        ),
    )(buffer)


def is_dense(rows, cap):
    return rows == 80 and cap == 96


def block_shape(rows, cap):
    return (64, 128) if is_dense(rows, cap) else (rows + 8, cap)


def store_block(ref, d, block, rows):
    cap = block.shape[1]
    if not is_dense(rows, cap):
        ref[d, : block.shape[0], :] = block
        return
    ref[d, :, :cap] = block[:64]
    ref[d, 48:, cap:] = jnp.zeros((16, 32), jnp.float32)
    for j in range(3):
        ref[d, 16 * j : 16 * j + 16, cap:] = block[64:80, 32 * j : 32 * j + 32]
        if block.shape[0] > rows:
            ref[d, 48 + j : 49 + j, cap:] = block[80:81, 32 * j : 32 * j + 32]


def load_block(ref, d, rows, cap):
    if not is_dense(rows, cap):
        return ref[d, :rows, :]
    tail = jnp.concatenate([ref[d, 16 * j : 16 * j + 16, cap:] for j in range(3)], axis=1)
    return jnp.concatenate([ref[d, :, :cap], tail], axis=0)


def load_tags(ref, d, rows, cap):
    if not is_dense(rows, cap):
        return ref[d, rows : rows + 1, :]
    return jnp.concatenate([ref[d, 48 + j : 49 + j, cap:] for j in range(3)], axis=1)


def swap(bufs, make, use, rows):
    sent, held, send, recv = bufs
    count = sent.shape[0]
    me = lax.axis_index("dom")

    def copy(i, source, target, other):
        return pltpu.make_async_remote_copy(
            src_ref=sent.at[source], dst_ref=held.at[target], send_sem=send.at[i],
            recv_sem=recv.at[i], device_id={"dom": other}, device_id_type=MESH,
        )

    def out(i):
        other = lax.rem(me + i, count)
        store_block(sent, other, make(other), rows)
        copy(i, other, me, other).start()

    def back(i):
        other = lax.rem(me + count - i, count)
        copy(i, other, other, other).wait_recv()
        use(other)

    def drain(i):
        other = lax.rem(me + i, count)
        copy(i, other, me, other).wait_send()

    each(1, count, out)
    store_block(held, me, make(me), rows)
    use(me)
    each(1, count, back)
    each(1, count, drain)


def partners(count):
    me = lax.axis_index("dom")
    return [lax.rem(me + i, count) for i in range(1, count)]


def split_quarters(acc, out):
    quarter = out.shape[2]
    for q in range(out.shape[0]):
        out[q] = acc[:, q * quarter : (q + 1) * quarter]


def first_in_kernel(cap, rhs, ids, places, arrived, out, acc, *bufs):
    rows, slots = rhs.shape
    count = arrived.shape[0]
    greet("dom", partners(count))
    if slots & (slots - 1) == 0:
        owner = lax.shift_right_logical(ids[...], slots.bit_length() - 1)
    else:
        owner = lax.div(ids[...], slots)
    within = ids[...] - owner * slots
    wide = max(count, 8)
    mine = lax.broadcasted_iota(jnp.int32, (wide, slots), 0) == jnp.broadcast_to(owner, (wide, slots))
    mine = mine.astype(jnp.float32)
    shape = (slots, slots)
    before = lax.broadcasted_iota(jnp.int32, shape, 0) < lax.broadcasted_iota(jnp.int32, shape, 1)
    ahead = lax.dot_general(
        mine, before.astype(jnp.float32), NN, preferred_element_type=jnp.float32
    )
    rank = jnp.sum(ahead * mine, axis=0, keepdims=True).astype(jnp.int32)
    places[...] = owner * cap + rank
    tags = jnp.broadcast_to((within + 1).astype(jnp.float32), (8, slots))
    full = jnp.concatenate([rhs[...], tags], axis=0)
    acc[...] = jnp.zeros_like(acc)

    def make(d):
        return dot(full, place_hot(places[...], cap, d), NT)

    def use(d):
        row = load_tags(bufs[1], d, rows, cap).astype(jnp.int32) - 1
        arrived[d] = row
        acc[...] += dot(load_block(bufs[1], d, rows, cap), line_hot(row, slots), NT)

    swap(bufs, make, use, rows)
    split_quarters(acc, out)


def second_in_kernel(
    cap, rhs, lateral, first, places, arrived, out, acc, low_edge, high_edge, edge_send, edge_recv, *bufs
):
    rows, slots = rhs.shape
    count = arrived.shape[0]
    me = lax.axis_index("dom")
    right, left = lax.rem(me + 1, count), lax.rem(me + count - 1, count)
    greet("dom", partners(count))
    copies = [
        pltpu.make_async_remote_copy(
            src_ref=first.at[:, pl.ds(start, 128)], dst_ref=edge, send_sem=edge_send.at[i],
            recv_sem=edge_recv.at[i], device_id={"dom": other}, device_id_type=MESH,
        )
        for i, (start, edge, other) in enumerate(
            ((slots - 128, low_edge, right), (0, high_edge, left))
        )
    ]
    for copy in copies:
        copy.start()
    acc[...] = jnp.zeros_like(acc)
    for copy in copies:
        copy.wait()
    low = jnp.where(me == 0, 0.0, low_edge[:, 127:128])
    high = jnp.where(me == count - 1, 0.0, high_edge[:, 0:1])
    lane = lax.broadcasted_iota(jnp.int32, (rows, slots), 1)
    here = first[...]
    below = jnp.where(lane == 0, jnp.broadcast_to(low, here.shape), pltpu.roll(here, 1, 1))
    above = jnp.where(
        lane == slots - 1, jnp.broadcast_to(high, here.shape), pltpu.roll(here, slots - 1, 1)
    )
    residual = rhs[...] + lateral[...] * (below + above)

    def make(d):
        return dot(residual, place_hot(places[...], cap, d), NT)

    def use(d):
        acc[...] += dot(load_block(bufs[1], d, rows, cap), line_hot(arrived[d], slots), NT)

    swap(bufs, make, use, rows)
    split_quarters(acc, out)


def home_kernel(cap, returned, arrived, places, out, *bufs):
    rows, slots = out.shape
    greet("dom", partners(arrived.shape[0]))
    lines = jnp.concatenate([returned[q] for q in range(returned.shape[0])], axis=1)
    out[...] = jnp.zeros_like(out)

    def make(d):
        return dot(lines, line_hot(arrived[d], slots), NN)

    def use(d):
        out[...] += dot(load_block(bufs[1], d, rows, cap), place_hot(places[...], cap, d), NN)

    swap(bufs, make, use, rows)


def body(rhs, lateral, piece_line, lower, diag_blocks, upper):
    fields, piece, line_dev = rhs.shape
    n_dom, n_sub = lax.axis_size("dom"), lax.axis_size("sub")
    mean_load = line_dev // n_dom
    cap = mean_load + (mean_load + 1) // 2
    rows = fields * piece
    f32 = lambda *shape: jax.ShapeDtypeStruct(shape, jnp.float32)
    i32 = lambda *shape: jax.ShapeDtypeStruct(shape, jnp.int32)
    rhs = rhs.reshape(rows, line_dev)
    lateral = lateral.reshape(rows, line_dev)
    acc = pltpu.VMEM((rows, line_dev), jnp.float32)
    bufs = [pltpu.VMEM((n_dom,) + block_shape(rows, cap), jnp.float32)] * 2
    bufs += [pltpu.SemaphoreType.DMA((n_dom,))] * 2
    quarters = f32(n_sub, rows, line_dev // n_sub)

    def remote(number):
        return pltpu.CompilerParams(
            vmem_limit_bytes=40 * 1024 * 1024, collective_id=number, has_side_effects=True
        )

    fac = factor(lower, diag_blocks, upper)
    places, arrived, sorted_first = call(
        functools.partial(first_in_kernel, cap),
        [i32(1, line_dev), i32(n_dom, 1, cap), quarters],
        rhs, piece_line, scratch=[acc] + bufs, params=remote(0),
    )

    def finish(given):
        solved = solve(fac, exchange(given, "sub", 2))
        return call(
            functools.partial(home_kernel, cap), f32(rows, line_dev),
            exchange(solved, "sub", 2), arrived, places, scratch=bufs, params=remote(4),
        )

    first = finish(sorted_first)
    edges = [pltpu.VMEM((rows, 128), jnp.float32)] * 2 + [pltpu.SemaphoreType.DMA((2,))] * 2
    sorted_second = call(
        functools.partial(second_in_kernel, cap), quarters, rhs, lateral, first, places, arrived,
        scratch=[acc] + edges + bufs, params=remote(1),
    )
    return finish(sorted_second).reshape(fields, piece, line_dev)


def solution(mesh):
    placed = (
        P(None, "sub", "dom"),
        P(None, "sub", "dom"),
        P("sub", "dom"),
        P(None, None, None, ("dom", "sub")),
        P(None, None, None, ("dom", "sub")),
        P(None, None, None, ("dom", "sub")),
    )
    return jax.shard_map(
        body, mesh=mesh, in_specs=placed, out_specs=P(None, "sub", "dom"), check_vma=False
    )
```
